512 devices in a mesh: af: 32 (over z_lo, x, core), sa: 16 (over z_hi, y).
Axes of the slice: x: 4, y: 8, z: 8 (z_hi: 2, z_lo: 4; z = z_hi * 4 + z_lo), core: 2. Of those that a mesh axis runs over, the one named last changes fastest.
Arguments:
- spatial_qkv: bfloat16 [32, 32, 80, 3456], P('af', None, 'sa'), may hold values from -9 to 9, as said below
- residual: bfloat16 [32, 32, 80, 1152], P('af', None, 'sa'), may hold values from -6 to 6
- gate: float32 [1152], replicated, may hold values from 1 to 4
- out_weight: bfloat16 [1152, 1152], P('af'), may hold values from -0.1875 to 0.1875
- temporal_weight: bfloat16 [1152, 3456], P('af'), may hold values from -2 to 2, as said below
Outputs:
- attended: bfloat16 [32, 32, 80, 1152], P('af', None, 'sa')
The draws below stay inside these ranges and needn't reach their ends.
Inputs may be any that keep to these rules, and one draw needn't show every extreme that they name: `spatial_qkv`: each token's last dimension holds, head after head, that head's query, key and value of 72 entries each. `temporal_weight`: each column block of 216 belongs to one head, in the order query, key, value.
All inputs are finite; a program needn't handle non-finite values.
Results may differ from the reference program's by a relative error of at most 0.029.
Values may be sent and summed in bfloat16 or wider, within the bound.
A program may use at most 128 MiB of HBM per device.

```python
import math
import jax
import jax.numpy as jnp
from jax import lax

D = 1152
HEADS = 16
HD = 72
ROWS = 32
COLS = 80
FRAMES = 32


def draw_spatial_qkv(key, part):
    key = jax.random.fold_in(key, 11)
    first = jax.random.fold_in(key, 0)
    full_shape = (FRAMES, ROWS, COLS, HEADS, 3, HD)
    spread = jnp.array([1.4, 1.4, 1.0], jnp.float32).reshape(1, 1, 1, 1, 3, 1)
    drawn = jnp.clip(jax.random.normal(first, full_shape, jnp.float32), -6.0, 6.0) * spread
    return drawn.reshape(FRAMES, ROWS, COLS, HEADS * 3 * HD).astype(jnp.bfloat16)


def draw_temporal_weight(key, part):
    key = jax.random.fold_in(key, 23)
    first = jax.random.fold_in(key, 0)
    full_shape = (D, HEADS, 3, HD)
    drawn = jnp.clip(jax.random.normal(first, full_shape, jnp.float32), -6.0, 6.0)
    return (drawn / math.sqrt(D)).reshape(D, 3 * D).astype(jnp.bfloat16)


def level_of(own_key, shape, cuts, smallest, largest):
    loudness, own = 1.0, jax.random.fold_in(own_key, 6)
    for position, shards_of in cuts:
        steps = jnp.exp(jax.random.uniform(jax.random.fold_in(own, position), (shards_of,), jnp.float32, smallest / len(cuts), largest / len(cuts)))
        loudness = loudness * jnp.repeat(steps, shape[position] // shards_of).reshape([-1 if axis == position else 1 for axis in range(len(shape))])
    return loudness


def normal_values(key, shape, width, bound, shards=(), held_as=jnp.bfloat16):
    entries = width * jax.random.normal(key, shape, jnp.float32)
    if shards:
        entries = entries * level_of(key, shape, shards, -0.22, 0.18)
    return jnp.clip(entries, -bound, bound).astype(held_as)


def setup_inputs(seed: int = 0) -> dict:
    splits = jax.random.split(jax.random.key(seed), 6)
    return {
        "spatial_qkv": draw_spatial_qkv(jax.random.fold_in(splits[5], 71), 0),
        "residual": normal_values(splits[1], (FRAMES, ROWS, COLS, D), 1.0, 6.0, ((0, 32), (2, 16))),
        "gate": jnp.clip(jax.random.uniform(splits[2], (D,), jnp.float32, 1.0, 4.0), 1.0, 4.0),
        "out_weight": normal_values(splits[3], (D, D), D ** -0.5, 0.1875, ((0, 32),)),
        "temporal_weight": draw_temporal_weight(jax.random.fold_in(splits[5], 71), 0),
    }


norm_epsilon = 1e-06

def normalize(values):
    average = lax.optimization_barrier(jnp.mean(values, axis=-1, keepdims=True))
    centred = values - average
    variance = lax.optimization_barrier(jnp.mean(centred * centred, axis=-1, keepdims=True))
    return centred * lax.rsqrt(variance + norm_epsilon)

def softmax_rows(scores):
    highest = lax.optimization_barrier(jnp.max(scores, axis=-1, keepdims=True))
    powers = jnp.exp(scores - highest)
    return powers / lax.optimization_barrier(jnp.sum(powers, axis=-1, keepdims=True))

def spatial_head(triple):
    inverse_root = 1.0 / math.sqrt(HD)
    scores = jnp.dot(triple[0], triple[1].T, preferred_element_type=jnp.float32) * inverse_root
    weights = softmax_rows(scores).astype(jnp.bfloat16)
    return jnp.dot(weights, triple[2], preferred_element_type=jnp.float32).astype(jnp.bfloat16)

def temporal_head(triple):
    inverse_root = 1.0 / math.sqrt(HD)
    queries = triple[0].astype(jnp.float32)
    keys_all = triple[1].astype(jnp.float32)
    values_all = triple[2].astype(jnp.float32)
    scores = jnp.einsum('tfd,tgd->tfg', queries, keys_all) * inverse_root
    weights = softmax_rows(scores).astype(jnp.bfloat16)
    mixed = jnp.einsum('tfg,tgd->tfd', weights.astype(jnp.float32), values_all)
    return mixed.astype(jnp.bfloat16)

def reference(spatial_qkv, residual, gate, out_weight, temporal_weight):
    token_count = ROWS * COLS
    grouped = spatial_qkv.reshape(FRAMES, token_count, HEADS, 3, HD)
    by_head = jnp.transpose(grouped, (0, 2, 3, 1, 4)).reshape(FRAMES * HEADS, 3, token_count, HD)
    spatial = lax.map(spatial_head, by_head)
    spatial = spatial.reshape(FRAMES, HEADS, token_count, HD).transpose(0, 2, 1, 3).reshape(FRAMES * token_count, D)
    projected = jnp.dot(spatial, out_weight, preferred_element_type=jnp.float32)
    hidden = (residual.reshape(FRAMES * token_count, D).astype(jnp.float32) + gate * projected).astype(jnp.bfloat16)
    normed = normalize(hidden.astype(jnp.float32)).astype(jnp.bfloat16)
    temporal = jnp.dot(normed, temporal_weight, preferred_element_type=jnp.float32).astype(jnp.bfloat16)
    temporal = temporal.reshape(FRAMES, token_count, HEADS, 3, HD)
    per_head = jnp.transpose(temporal, (2, 3, 1, 0, 4))
    attended = lax.map(temporal_head, per_head)
    return jnp.transpose(attended, (2, 1, 0, 3)).reshape(FRAMES, ROWS, COLS, D)
```

```python
import math

import jax
import jax.numpy as jnp
from jax import lax
from jax.experimental import pallas as pl
from jax.experimental.pallas import tpu as pltpu
from jax.sharding import PartitionSpec as P

D = 1152
HEADS = 16
HD = 72
TRIPLE = 3 * HD
EPSILON = 1e-06
SCALE = 1.0 / math.sqrt(HD)
EXP2_SCALE = SCALE * math.log2(math.e)
MESH = pl.DeviceIdType.MESH
F32 = jnp.float32
BF16 = jnp.bfloat16
VMEM_LIMIT = 56 * 1024 * 1024


def greet(axis, count):
    me = lax.axis_index(axis)
    barrier = pltpu.get_barrier_semaphore()

    def signal(step, carry):
        pl.semaphore_signal(
            barrier, inc=1, device_id={axis: lax.rem(me + step, count)}, device_id_type=MESH
        )
        return carry

    lax.fori_loop(1, count, signal, 0)
    return barrier


def exchange(axis, count, source, target, send_sem, recv_sem):
    me = lax.axis_index(axis)

    def copy(peer):
        return pltpu.make_async_remote_copy(
            src_ref=source.at[peer],
            dst_ref=target.at[me],
            send_sem=send_sem.at[peer],
            recv_sem=recv_sem.at[me],
            device_id={axis: peer},
            device_id_type=MESH,
        )

    def arrival(peer):
        return pltpu.make_async_remote_copy(
            src_ref=source.at[peer],
            dst_ref=target.at[peer],
            send_sem=send_sem.at[peer],
            recv_sem=recv_sem.at[peer],
            device_id={axis: peer},
            device_id_type=MESH,
        )

    return copy, arrival


def spatial_kernel(
    x_ref, o_ref, send, recv, keys, osend, orecv, send_sem, recv_sem, osend_sem, orecv_sem
):
    count = HEADS
    tokens = x_ref.shape[0]
    me = lax.axis_index("sa")
    barrier = greet("sa", count)
    for head in range(count):
        send[head, :, 0:TRIPLE] = x_ref[:, head * TRIPLE : (head + 1) * TRIPLE]
        send[head, :, TRIPLE:256] = jnp.ones((tokens, 256 - TRIPLE), BF16)
    pl.semaphore_wait(barrier, count - 1)
    copy, arrival = exchange("sa", count, send, recv, send_sem, recv_sem)
    ocopy, oarrival = exchange("sa", count, osend, orecv, osend_sem, orecv_sem)

    def start(step, carry):
        copy(lax.rem(me + step, count)).start()
        return carry

    lax.fori_loop(1, count, start, 0)
    recv[me] = send[me]
    lane = lax.broadcasted_iota(jnp.int32, (tokens, 128), 1)

    def take(source):
        block = recv[source]
        key = jnp.concatenate(
            [block[:, HD : 2 * HD], jnp.zeros((tokens, 128 - HD), BF16)], axis=1
        )
        keys[source] = key

    take(me)

    def receive(step, carry):
        source = lax.rem(me + step, count)
        arrival(source).wait_recv()
        take(source)
        return carry

    lax.fori_loop(1, count, receive, 0)

    def attend(step, carry):
        owner = lax.rem(me + step, count)
        queries = recv[owner, :, 0:128]
        every = keys[...].reshape(count * tokens, 128)
        values = recv[:, :, 128:256].reshape(count * tokens, 128)
        scores = lax.dot_general(
            queries, every, (((1,), (1,)), ((), ())), preferred_element_type=F32
        )
        highest = jnp.max(scores, axis=-1, keepdims=True)
        powers = jnp.exp2((scores - highest) * EXP2_SCALE).astype(BF16)
        mixed = jnp.dot(powers, values, preferred_element_type=F32)
        total = mixed[:, 88:89]
        osend[owner] = (mixed / total).astype(BF16)

        @pl.when(step < count)
        def _():
            ocopy(owner).start()

        return carry

    lax.fori_loop(1, count + 1, attend, 0)
    orecv[me] = osend[me]

    def finish(step, carry):
        peer = lax.rem(me + step, count)
        oarrival(peer).wait_recv()
        return carry

    lax.fori_loop(1, count, finish, 0)
    for head in range(count):
        o_ref[:, head * HD : (head + 1) * HD] = orecv[head, :, 16 : 16 + HD]

    def drain(step, carry):
        peer = lax.rem(me + step, count)
        copy(peer).wait_send()
        ocopy(peer).wait_send()
        return carry

    lax.fori_loop(1, count, drain, 0)


def spatial(x):
    tokens = x.shape[0]
    count = HEADS
    return pl.pallas_call(
        spatial_kernel,
        out_shape=jax.ShapeDtypeStruct((tokens, D), BF16),
        in_specs=[pl.BlockSpec(memory_space=pltpu.VMEM)],
        out_specs=pl.BlockSpec(memory_space=pltpu.VMEM),
        scratch_shapes=[
            pltpu.VMEM((count, tokens, 256), BF16),
            pltpu.VMEM((count, tokens, 256), BF16),
            pltpu.VMEM((count, tokens, 128), BF16),
            pltpu.VMEM((count, tokens, 128), BF16),
            pltpu.VMEM((count, tokens, 128), BF16),
            pltpu.SemaphoreType.DMA((count,)),
            pltpu.SemaphoreType.DMA((count,)),
            pltpu.SemaphoreType.DMA((count,)),
            pltpu.SemaphoreType.DMA((count,)),
        ],
        compiler_params=pltpu.CompilerParams(
            collective_id=0, has_side_effects=True, vmem_limit_bytes=VMEM_LIMIT
        ),
    )(x)


ROWS = 32
COLS = 5
SLABS = 48


def to_slabs(slabs, values):
    for col in range(COLS):
        for part in range(D // 128):
            slabs[:, col * 9 + part, :] = values[
                col * ROWS : (col + 1) * ROWS, part * 128 : (part + 1) * 128
            ]
    slabs[:, COLS * 9 : SLABS, :] = jnp.zeros((ROWS, SLABS - COLS * 9, 128), F32)


def from_slabs(target, slabs):
    for col in range(COLS):
        for part in range(D // 128):
            target[col * ROWS : (col + 1) * ROWS, part * 128 : (part + 1) * 128] = slabs[
                :, col * 9 + part, :
            ].astype(BF16)


def temporal_kernel(
    attn_ref, residual_ref, gate_ref, out_weight_ref, temporal_weight_ref, o_ref,
    slabs, send, recv, tokens_ref, qkv_ref, mixed_ref, osend, orecv,
    send_sem, recv_sem, osend_sem, orecv_sem,
):
    count = ROWS
    me = lax.axis_index("af")
    barrier = greet("af", count)
    projected = jnp.dot(attn_ref[...], out_weight_ref[...], preferred_element_type=F32)
    hidden = (residual_ref[...].astype(F32) + gate_ref[...] * projected).astype(BF16).astype(F32)
    average = jnp.mean(hidden, axis=-1, keepdims=True)
    centred = hidden - average
    variance = jnp.mean(centred * centred, axis=-1, keepdims=True)
    mixed_ref[...] = centred * lax.rsqrt(variance + EPSILON)
    to_slabs(slabs, mixed_ref)
    send[...] = slabs[...].astype(BF16)
    pl.semaphore_wait(barrier, count - 1)
    copy, arrival = exchange("af", count, send, recv, send_sem, recv_sem)
    ocopy, oarrival = exchange("af", count, osend, orecv, osend_sem, orecv_sem)

    def start(step, carry):
        copy(lax.rem(me + step, count)).start()
        return carry

    lax.fori_loop(1, count, start, 0)
    recv[me] = send[me]

    def receive(step, carry):
        arrival(lax.rem(me + step, count)).wait_recv()
        return carry

    lax.fori_loop(1, count, receive, 0)
    slabs[...] = recv[...].astype(F32)
    from_slabs(tokens_ref, slabs)
    qkv_ref[...] = jnp.dot(
        tokens_ref[...], temporal_weight_ref[...], preferred_element_type=F32
    ).astype(BF16)
    tokens = COLS * ROWS
    first = lax.broadcasted_iota(jnp.int32, (tokens, tokens), 0)
    second = lax.broadcasted_iota(jnp.int32, (tokens, tokens), 1)
    same = lax.shift_right_logical(first, 5) == lax.shift_right_logical(second, 5)
    for head in range(HEADS):
        base = head * TRIPLE
        queries = qkv_ref[:, base : base + HD]
        keys = qkv_ref[:, base + HD : base + 2 * HD]
        values = qkv_ref[:, base + 2 * HD : base + 3 * HD]
        scores = lax.dot_general(
            queries, keys, (((1,), (1,)), ((), ())), preferred_element_type=F32
        )
        scores = jnp.where(same, scores, -jnp.inf)
        highest = jnp.max(scores, axis=-1, keepdims=True)
        powers = jnp.exp2((scores - highest) * EXP2_SCALE)
        weights = (powers / jnp.sum(powers, axis=-1, keepdims=True)).astype(BF16)
        mixed_ref[:, head * HD : (head + 1) * HD] = jnp.dot(
            weights, values, preferred_element_type=F32
        )
    to_slabs(slabs, mixed_ref)
    osend[...] = slabs[...].astype(BF16)

    def ostart(step, carry):
        ocopy(lax.rem(me + step, count)).start()
        return carry

    lax.fori_loop(1, count, ostart, 0)
    orecv[me] = osend[me]

    def oreceive(step, carry):
        oarrival(lax.rem(me + step, count)).wait_recv()
        return carry

    lax.fori_loop(1, count, oreceive, 0)
    slabs[...] = orecv[...].astype(F32)
    from_slabs(o_ref, slabs)

    def drain(step, carry):
        peer = lax.rem(me + step, count)
        copy(peer).wait_send()
        ocopy(peer).wait_send()
        return carry

    lax.fori_loop(1, count, drain, 0)


def temporal(attn, residual, gate, out_weight, temporal_weight):
    tokens = attn.shape[0]
    count = ROWS
    return pl.pallas_call(
        temporal_kernel,
        out_shape=jax.ShapeDtypeStruct((tokens, D), BF16),
        in_specs=[pl.BlockSpec(memory_space=pltpu.VMEM)] * 5,
        out_specs=pl.BlockSpec(memory_space=pltpu.VMEM),
        scratch_shapes=[
            pltpu.VMEM((count, SLABS, 128), F32),
            pltpu.VMEM((count, SLABS, 128), BF16),
            pltpu.VMEM((count, SLABS, 128), BF16),
            pltpu.VMEM((tokens, D), BF16),
            pltpu.VMEM((tokens, 3 * D), BF16),
            pltpu.VMEM((tokens, D), F32),
            pltpu.VMEM((count, SLABS, 128), BF16),
            pltpu.VMEM((count, SLABS, 128), BF16),
            pltpu.SemaphoreType.DMA((count,)),
            pltpu.SemaphoreType.DMA((count,)),
            pltpu.SemaphoreType.DMA((count,)),
            pltpu.SemaphoreType.DMA((count,)),
        ],
        compiler_params=pltpu.CompilerParams(
            collective_id=1, has_side_effects=True, vmem_limit_bytes=VMEM_LIMIT
        ),
    )(attn, residual, gate, out_weight, temporal_weight)


def flat(values):
    return jnp.transpose(values, (0, 2, 1, 3)).reshape(-1, values.shape[-1])


def local(spatial_qkv, residual, gate, out_weight, temporal_weight):
    frames, rows, cols, _ = residual.shape
    shards = jnp.concatenate([out_weight, temporal_weight], axis=1)
    weights = lax.all_gather(shards, "af", axis=0, tiled=True)
    attn = spatial(flat(spatial_qkv))
    attended = temporal(
        attn, flat(residual), gate.reshape(1, D), weights[:, :D], weights[:, D:]
    )
    return jnp.transpose(attended.reshape(frames, cols, rows, D), (0, 2, 1, 3))


def solution(mesh):
    placed = (
        P("af", None, "sa", None),
        P("af", None, "sa", None),
        P(),
        P("af", None),
        P("af", None),
    )
    return jax.shard_map(
        local, mesh=mesh, in_specs=placed, out_specs=P("af", None, "sa", None), check_vma=False
    )
```

```python
import math

import jax
import jax.numpy as jnp
from jax import lax
from jax.experimental import pallas as pl
from jax.experimental.pallas import tpu as pltpu
from jax.sharding import PartitionSpec as P

D = 1152
HEADS = 16
HD = 72
TRIPLE = 3 * HD
EPSILON = 1e-06
SCALE = 1.0 / math.sqrt(HD)
EXP2_SCALE = SCALE * math.log2(math.e)
MESH = pl.DeviceIdType.MESH
F32 = jnp.float32
BF16 = jnp.bfloat16
VMEM_LIMIT = 60 * 1024 * 1024

ROWS = 32
COLS = 5
TOKENS = ROWS * COLS
SLABS = 48
PACKED = 96
UNIT = 80
BLOCK = 640
CHUNK = 256


def signal(barrier, device):
    pl.semaphore_signal(barrier, inc=1, device_id=device, device_id_type=MESH)


def exchange(axis, source, target, send_sem, recv_sem):
    me = lax.axis_index(axis)

    def describe(peer, slot):
        return pltpu.make_async_remote_copy(
            src_ref=source.at[peer],
            dst_ref=target.at[slot],
            send_sem=send_sem.at[peer],
            recv_sem=recv_sem.at[slot],
            device_id={axis: peer},
            device_id_type=MESH,
        )

    return lambda peer: describe(peer, me), lambda peer: describe(peer, peer)


def packed(values, base):
    top = jnp.concatenate(
        [values[0:64, base : base + HD], values[96:160, base : base + 56]], axis=1
    )
    bottom = jnp.concatenate(
        [
            values[64:96, base : base + HD],
            values[96:128, base + 56 : base + HD],
            values[128:160, base + 56 : base + HD],
            jnp.zeros((32, 24), values.dtype),
        ],
        axis=1,
    )
    return top, bottom


def unpacked(block):
    rest = jnp.zeros((32, 56), block.dtype)
    third = jnp.concatenate([block[0:32, HD:128], block[64:96, HD : HD + 16], rest], axis=1)
    fourth = jnp.concatenate(
        [block[32:64, HD:128], block[64:96, HD + 16 : HD + 32], rest], axis=1
    )
    return jnp.concatenate([block, third, fourth], axis=0)


def to_slabs(slabs, values):
    for col in range(COLS):
        for part in range(D // 128):
            slabs[:, col * 9 + part, :] = values[
                col * ROWS : (col + 1) * ROWS, part * 128 : (part + 1) * 128
            ]
    slabs[:, COLS * 9 : SLABS, :] = jnp.zeros((ROWS, SLABS - COLS * 9, 128), F32)


def from_slabs(target, slabs):
    for col in range(COLS):
        for part in range(D // 128):
            target[col * ROWS : (col + 1) * ROWS, part * 128 : (part + 1) * 128] = slabs[
                :, col * 9 + part, :
            ].astype(BF16)


def kernel(
    x_ref, residual_ref, gate_ref, out_ref, temporal_ref, o_ref,
    kv_send, kv_recv, q_send, q_recv, o_send, o_recv, queries, keys, values, attn,
    weights, stage_send, stage_recv,
    slabs, n_send, n_recv, wide, dense, qkv, t_send, t_recv,
    kv_ss, kv_rs, q_ss, q_rs, o_ss, o_rs, n_ss, n_rs, t_ss, t_rs,
    stage_ss, stage_rs, weight_rs, side_ss, depth_ss,
):
    af, sa = lax.axis_index("af"), lax.axis_index("sa")
    low, x, core = lax.div(af, 8), lax.rem(lax.div(af, 2), 4), lax.rem(af, 2)
    high, y = lax.div(sa, 8), lax.rem(sa, 8)
    z = high * 4 + low

    def along_z(step):
        there = lax.rem(z + step + 8, 8)
        return {
            "af": lax.rem(there, 4) * 8 + x * 2 + core,
            "sa": lax.div(there, 4) * 8 + y,
        }

    def along_x(step):
        return {"af": low * 8 + lax.rem(x + step + 4, 4) * 2 + core}

    sibling = {"af": af + 1 - 2 * core}

    barrier = pltpu.get_barrier_semaphore()

    def greet_sa(step, carry):
        signal(barrier, {"sa": lax.rem(sa + step, HEADS)})
        return carry

    def greet_af(step, carry):
        signal(barrier, {"af": lax.rem(af + step, ROWS)})
        return carry

    lax.fori_loop(1, HEADS, greet_sa, 0)
    for step in (1, -1, 2, -2):
        signal(barrier, along_z(step))
    lax.fori_loop(1, ROWS, greet_af, 0)

    kv_copy, kv_arrival = exchange("sa", kv_send, kv_recv, kv_ss, kv_rs)
    q_copy, q_arrival = exchange("sa", q_send, q_recv, q_ss, q_rs)
    o_copy, o_arrival = exchange("sa", o_send, o_recv, o_ss, o_rs)
    n_copy, n_arrival = exchange("af", n_send, n_recv, n_ss, n_rs)
    t_copy, t_arrival = exchange("af", t_send, t_recv, t_ss, t_rs)

    def place(u, p):
        return weights.at[
            pl.ds(pl.multiple_of(u * UNIT, 16), UNIT), pl.ds(pl.multiple_of(p * D, 128), D)
        ]

    def mine(j):
        return core + 2 * j

    def theirs(j):
        return 1 - core + 2 * j

    def weight_copy(u, p, sem, device):
        return pltpu.make_async_remote_copy(
            src_ref=place(u, p),
            dst_ref=place(u, p),
            send_sem=sem,
            recv_sem=weight_rs.at[u, p],
            device_id=device,
            device_id_type=MESH,
        )

    def right(u, j):
        return weight_copy(u, mine(j), side_ss.at[0, u, j], along_x(1))

    def left(u, j):
        return weight_copy(u, mine(j), side_ss.at[1, u, j], along_x(-1))

    def across(u, j):
        return weight_copy(u, mine(j), side_ss.at[2, u, j], sibling)

    def arrived(u, p):
        weight_copy(u, p, side_ss.at[0, u, 0], sibling).wait_recv()

    own = low * 4 + x

    def up(j):
        return weight_copy(own, mine(j), depth_ss.at[0, j], along_z(1))

    def down(j):
        return weight_copy(own, mine(j), depth_ss.at[1, j], along_z(-1))

    def far(j):
        return weight_copy(own, mine(j), depth_ss.at[2, j], along_z(2 if j == 0 else -2))

    def unit(low_step, x_step):
        return lax.rem(low + low_step, 4) * 4 + lax.rem(x + x_step, 4)

    def stage(j):
        return pltpu.make_async_remote_copy(
            src_ref=stage_send.at[theirs(j)],
            dst_ref=stage_recv.at[j],
            send_sem=stage_ss.at[j],
            recv_sem=stage_rs.at[j],
            device_id=sibling,
            device_id_type=MESH,
        )

    stage_send[0, 0:36, :] = out_ref[...]
    for p in range(3):
        stage_send[1 + p, 0:36, :] = temporal_ref[:, p * D : (p + 1) * D]
    for p in range(4):
        stage_send[p, 36:48, :] = jnp.zeros((12, D), BF16)

    for head in range(HEADS):
        base = head * TRIPLE
        for target, row, start in (
            (kv_send, 0, base + HD), (kv_send, PACKED, base + 2 * HD), (q_send, 0, base),
        ):
            top, bottom = packed(x_ref, start)
            target[head, row : row + 64, :] = top
            target[head, row + 64 : row + PACKED, :] = bottom

    pl.semaphore_wait(barrier, HEADS - 1 + ROWS - 1 + 4)
    for j in range(2):
        stage(j).start()

    def kv_start(step, carry):
        kv_copy(lax.rem(sa + step, HEADS)).start()
        return carry

    lax.fori_loop(1, HEADS, kv_start, 0)

    for j in range(2):
        stage(j).wait_recv()
        here = stage_send[mine(j), 0:36, :].astype(F32)
        there = stage_recv[j, 0:36, :].astype(F32)
        first = jnp.where(core == 0, here, there)
        second = jnp.where(core == 0, there, here)
        place(own, mine(j))[...] = jnp.concatenate(
            [first, second, jnp.zeros((8, D), F32)], axis=0
        ).astype(BF16)
        for copy in (right, left):
            copy(own, j).start()
        for copy in (up, down, far):
            copy(j).start()
        across(own, j).start()

    lane = lax.broadcasted_iota(jnp.int32, (TOKENS, 128), 1)

    def take(slot, block):
        key = unpacked(block[0:PACKED])
        value = unpacked(block[PACKED : 2 * PACKED])
        keys[slot] = jnp.where(lane < HD, key, jnp.zeros_like(key))
        values[slot] = jnp.where(lane < HD, value, jnp.ones_like(value))

    take(0, kv_send[sa])
    queries[0] = unpacked(q_send[sa])

    def receive(step, carry):
        source = lax.rem(sa + step, HEADS)
        kv_arrival(source).wait_recv()
        take(step, kv_recv[source])
        kv_copy(source).wait_send()
        q_copy(source).start()

        @pl.when(jnp.logical_and(lax.rem(step, 2) == 1, step >= 3))
        def _():
            turn = lax.div(step - 3, 2)
            @pl.when(turn < 6)
            def _():
                which = lax.div(turn, 2)
                j = lax.rem(turn, 2)
                u = unit(jnp.where(which == 0, 1, jnp.where(which == 1, 3, 2)), 0)
                arrived(u, mine(j))
                right(u, j).start()
                left(u, j).start()
                across(u, j).start()

        return carry

    lax.fori_loop(1, HEADS, receive, 0)

    slots = BLOCK // TOKENS

    def attend(block, carry):
        def query(slot):
            source = lax.rem(sa + slot, HEADS)
            q_arrival(source).wait_recv()
            queries[slot] = unpacked(q_recv[source])

        for index in range(slots):
            slot = block * slots + index
            if index == 0:
                pl.when(block > 0)(lambda: query(slot))
            else:
                query(slot)
        rows = queries[pl.ds(block * slots, slots)].reshape(BLOCK, 128)
        all_keys = keys[...].reshape(HEADS * TOKENS, 128)
        all_values = values[...].reshape(HEADS * TOKENS, 128)
        highest = total = None
        for start in range(0, HEADS * TOKENS, CHUNK):
            scores = lax.dot_general(
                rows, all_keys[start : start + CHUNK], (((1,), (1,)), ((), ())),
                preferred_element_type=F32,
            )
            top = jnp.max(scores, axis=-1, keepdims=True)
            if highest is not None:
                top = jnp.maximum(highest, top)
            powers = jnp.exp2((scores - top) * EXP2_SCALE).astype(BF16)
            mixed = jnp.dot(
                powers, all_values[start : start + CHUNK], preferred_element_type=F32
            )
            if highest is not None:
                mixed = mixed + total * jnp.exp2((highest - top) * EXP2_SCALE)
            highest, total = top, mixed
        result = (total / total[:, HD : HD + 1]).astype(BF16)
        for index in range(slots):
            slot = block * slots + index
            owner = lax.rem(sa + slot, HEADS)
            top, bottom = packed(result[index * TOKENS : (index + 1) * TOKENS], 0)
            o_send[owner, 0:64, :] = top
            o_send[owner, 64:PACKED, :] = bottom
            if index == 0:
                pl.when(block > 0)(lambda: o_copy(owner).start())
            else:
                o_copy(owner).start()
        low_step = jnp.where(block == 2, 3, jnp.where(block == 3, 2, block))
        before, after = unit(low_step, 3), unit(low_step, 1)
        arrived(before, mine(0))
        right(before, 0).start()
        across(before, 0).start()
        arrived(after, mine(0))
        across(after, 0).start()
        arrived(after, mine(1))
        left(after, 1).start()
        across(after, 1).start()
        arrived(before, mine(1))
        across(before, 1).start()
        return carry

    lax.fori_loop(0, HEADS // slots, attend, 0)

    def opposite(j):
        def step(turn, carry):
            u = unit(turn, 2)
            arrived(u, mine(j))
            across(u, j).start()
            return carry

        lax.fori_loop(0, 4, step, 0)

    def swapped(j):
        def step(u, carry):
            arrived(u, theirs(j))
            return carry

        lax.fori_loop(0, 16, step, 0)

    o_recv[sa] = o_send[sa]

    def o_receive(step, carry):
        o_arrival(lax.rem(sa + step, HEADS)).wait_recv()
        return carry

    lax.fori_loop(1, HEADS, o_receive, 0)
    for head in range(HEADS):
        attn[:, head * UNIT : head * UNIT + HD] = unpacked(o_recv[head])[:, 0:HD]
        attn[:, head * UNIT + HD : (head + 1) * UNIT] = jnp.zeros((TOKENS, UNIT - HD), BF16)
    opposite(0)
    swapped(0)
    projected = jnp.dot(attn[...], weights[:, 0:D], preferred_element_type=F32)
    hidden = (residual_ref[...].astype(F32) + gate_ref[...] * projected).astype(BF16).astype(F32)
    average = jnp.mean(hidden, axis=-1, keepdims=True)
    centred = hidden - average
    variance = jnp.mean(centred * centred, axis=-1, keepdims=True)
    wide[...] = centred * lax.rsqrt(variance + EPSILON)
    to_slabs(slabs, wide)
    n_send[...] = slabs[...].astype(BF16)

    def n_start(step, carry):
        n_copy(lax.rem(af + step, ROWS)).start()
        return carry

    lax.fori_loop(1, ROWS, n_start, 0)
    n_recv[af] = n_send[af]
    opposite(1)

    def n_receive(step, carry):
        n_arrival(lax.rem(af + step, ROWS)).wait_recv()
        return carry

    lax.fori_loop(1, ROWS, n_receive, 0)
    slabs[...] = n_recv[...].astype(F32)
    from_slabs(dense, slabs)
    for head in range(HEADS):
        attn[:, head * UNIT : head * UNIT + HD] = dense[:, head * HD : (head + 1) * HD]
    swapped(1)
    qkv[...] = jnp.dot(attn[...], weights[:, D:], preferred_element_type=F32).astype(BF16)

    first = lax.broadcasted_iota(jnp.int32, (TOKENS, TOKENS), 0)
    second = lax.broadcasted_iota(jnp.int32, (TOKENS, TOKENS), 1)
    same = lax.shift_right_logical(first, 5) == lax.shift_right_logical(second, 5)
    for head in range(HEADS):
        base = head * TRIPLE
        scores = lax.dot_general(
            qkv[:, base : base + HD], qkv[:, base + HD : base + 2 * HD],
            (((1,), (1,)), ((), ())), preferred_element_type=F32,
        )
        scores = jnp.where(same, scores, -jnp.inf)
        highest = jnp.max(scores, axis=-1, keepdims=True)
        powers = jnp.exp2((scores - highest) * EXP2_SCALE)
        shares = (powers / jnp.sum(powers, axis=-1, keepdims=True)).astype(BF16)
        wide[:, head * HD : (head + 1) * HD] = jnp.dot(
            shares, qkv[:, base + 2 * HD : base + 3 * HD], preferred_element_type=F32
        )
    to_slabs(slabs, wide)
    t_send[...] = slabs[...].astype(BF16)

    def t_start(step, carry):
        t_copy(lax.rem(af + step, ROWS)).start()
        return carry

    lax.fori_loop(1, ROWS, t_start, 0)
    t_recv[af] = t_send[af]

    def drain_sa(step, carry):
        peer = lax.rem(sa + step, HEADS)
        q_copy(peer).wait_send()
        o_copy(peer).wait_send()
        return carry

    lax.fori_loop(1, HEADS, drain_sa, 0)
    for j in range(2):
        stage(j).wait_send()
        for copy in (up, down, far):
            copy(j).wait_send()

    def drain_sides(turn, carry):
        for j in range(2):
            right(unit(turn, 0), j).wait_send()
            left(unit(turn, 0), j).wait_send()
            for x_step in range(4):
                across(unit(turn, x_step), j).wait_send()
        right(unit(turn, 3), 0).wait_send()
        left(unit(turn, 1), 1).wait_send()
        return carry

    lax.fori_loop(0, 4, drain_sides, 0)

    def t_receive(step, carry):
        peer = lax.rem(af + step, ROWS)
        n_copy(peer).wait_send()
        t_arrival(peer).wait_recv()
        return carry

    lax.fori_loop(1, ROWS, t_receive, 0)
    slabs[...] = t_recv[...].astype(F32)
    from_slabs(o_ref, slabs)

    def drain_af(step, carry):
        t_copy(lax.rem(af + step, ROWS)).wait_send()
        return carry

    lax.fori_loop(1, ROWS, drain_af, 0)


def flat(values):
    return jnp.transpose(values, (0, 2, 1, 3)).reshape(-1, values.shape[-1])


def local(spatial_qkv, residual, gate, out_weight, temporal_weight):
    frames, rows, cols, _ = residual.shape
    dma = pltpu.SemaphoreType.DMA
    attended = pl.pallas_call(
        kernel,
        out_shape=jax.ShapeDtypeStruct((TOKENS, D), BF16),
        in_specs=[pl.BlockSpec(memory_space=pltpu.VMEM)] * 5,
        out_specs=pl.BlockSpec(memory_space=pltpu.VMEM),
        scratch_shapes=[
            pltpu.VMEM((HEADS, 2 * PACKED, 128), BF16),
            pltpu.VMEM((HEADS, 2 * PACKED, 128), BF16),
            pltpu.VMEM((HEADS, PACKED, 128), BF16),
            pltpu.VMEM((HEADS, PACKED, 128), BF16),
            pltpu.VMEM((HEADS, PACKED, 128), BF16),
            pltpu.VMEM((HEADS, PACKED, 128), BF16),
            pltpu.VMEM((HEADS, TOKENS, 128), BF16),
            pltpu.VMEM((HEADS, TOKENS, 128), BF16),
            pltpu.VMEM((HEADS, TOKENS, 128), BF16),
            pltpu.VMEM((TOKENS, HEADS * UNIT), BF16),
            pltpu.VMEM((HEADS * UNIT, 4 * D), BF16),
            pltpu.VMEM((4, 48, D), BF16),
            pltpu.VMEM((2, 48, D), BF16),
            pltpu.VMEM((ROWS, SLABS, 128), F32),
            pltpu.VMEM((ROWS, SLABS, 128), BF16),
            pltpu.VMEM((ROWS, SLABS, 128), BF16),
            pltpu.VMEM((TOKENS, D), F32),
            pltpu.VMEM((TOKENS, D), BF16),
            pltpu.VMEM((TOKENS, 3 * D), BF16),
            pltpu.VMEM((ROWS, SLABS, 128), BF16),
            pltpu.VMEM((ROWS, SLABS, 128), BF16),
        ]
        + [dma((HEADS,))] * 6
        + [dma((ROWS,))] * 4
        + [dma((2,)), dma((2,)), dma((16, 4)), dma((3, 16, 2)), dma((3, 2))],
        compiler_params=pltpu.CompilerParams(
            collective_id=0, has_side_effects=True, vmem_limit_bytes=VMEM_LIMIT
        ),
    )(flat(spatial_qkv), flat(residual), gate.reshape(1, D), out_weight, temporal_weight)
    return jnp.transpose(attended.reshape(frames, cols, rows, D), (0, 2, 1, 3))


def solution(mesh):
    placed = (
        P("af", None, "sa", None),
        P("af", None, "sa", None),
        P(),
        P("af", None),
        P("af", None),
    )
    return jax.shard_map(
        local, mesh=mesh, in_specs=placed, out_specs=P("af", None, "sa", None), check_vma=False
    )
```

```python
import math

import jax
import jax.numpy as jnp
from jax import lax
from jax.experimental import pallas as pl
from jax.experimental.pallas import tpu as pltpu
from jax.sharding import PartitionSpec as P

D = 1152
HEADS = 16
HD = 72
TRIPLE = 3 * HD
EPSILON = 1e-06
SCALE = 1.0 / math.sqrt(HD)
EXP2_SCALE = SCALE * math.log2(math.e)
MESH = pl.DeviceIdType.MESH
F32 = jnp.float32
BF16 = jnp.bfloat16
VMEM_LIMIT = 60 * 1024 * 1024

ROWS = 32
COLS = 5
TOKENS = ROWS * COLS
SLABS = 48
PACKED = 96
UNIT = 80
BLOCK = 640
CHUNK = 256
FIRST = (0, 10, 18)
TILES = (5, 4, 9)
PIECES = range(3)
GROUP = 4 * UNIT


def signal(barrier, device):
    pl.semaphore_signal(barrier, inc=1, device_id=device, device_id_type=MESH)


def exchange(axis, source, target, send_sem, recv_sem):
    me = lax.axis_index(axis)

    def describe(peer, slot):
        return pltpu.make_async_remote_copy(
            src_ref=source.at[peer],
            dst_ref=target.at[slot],
            send_sem=send_sem.at[peer],
            recv_sem=recv_sem.at[slot],
            device_id={axis: peer},
            device_id_type=MESH,
        )

    return lambda peer: describe(peer, me), lambda peer: describe(peer, peer)


def packed(values, base):
    top = jnp.concatenate(
        [values[0:64, base : base + HD], values[96:160, base : base + 56]], axis=1
    )
    bottom = jnp.concatenate(
        [
            values[64:96, base : base + HD],
            values[96:128, base + 56 : base + HD],
            values[128:160, base + 56 : base + HD],
            jnp.zeros((32, 24), values.dtype),
        ],
        axis=1,
    )
    return top, bottom


def unpacked(block):
    rest = jnp.zeros((32, 56), block.dtype)
    third = jnp.concatenate([block[0:32, HD:128], block[64:96, HD : HD + 16], rest], axis=1)
    fourth = jnp.concatenate(
        [block[32:64, HD:128], block[64:96, HD + 16 : HD + 32], rest], axis=1
    )
    return jnp.concatenate([block, third, fourth], axis=0)


def to_slabs(slabs, values):
    for col in range(COLS):
        for part in range(D // 128):
            slabs[:, col * 9 + part, :] = values[
                col * ROWS : (col + 1) * ROWS, part * 128 : (part + 1) * 128
            ]
    slabs[:, COLS * 9 : SLABS, :] = jnp.zeros((ROWS, SLABS - COLS * 9, 128), F32)


def from_slabs(target, slabs):
    for col in range(COLS):
        for part in range(D // 128):
            target[col * ROWS : (col + 1) * ROWS, part * 128 : (part + 1) * 128] = slabs[
                :, col * 9 + part, :
            ].astype(BF16)


def kernel(
    x_ref, residual_ref, gate_ref, out_ref, temporal_ref, o_ref,
    kv_send, kv_recv, q_send, q_recv, o_send, o_recv, queries, keys, values, attn,
    weights, stage_send, stage_recv,
    slabs, n_send, n_recv, wide, dense, qkv, t_send, t_recv,
    kv_ss, kv_rs, q_ss, q_rs, o_ss, o_rs, n_ss, n_rs, t_ss, t_rs,
    stage_ss, stage_rs, depth_ss, side_ss, unit_rs, pair_ss, pair_rs,
):
    af, sa = lax.axis_index("af"), lax.axis_index("sa")
    low, x, core = lax.div(af, 8), lax.rem(lax.div(af, 2), 4), lax.rem(af, 2)
    high, y = lax.div(sa, 8), lax.rem(sa, 8)
    z = high * 4 + low

    def along_z(step):
        there = lax.rem(z + step + 8, 8)
        return {
            "af": lax.rem(there, 4) * 8 + x * 2 + core,
            "sa": lax.div(there, 4) * 8 + y,
        }

    def along_x(step):
        return {"af": low * 8 + lax.rem(x + step + 4, 4) * 2 + core}

    sibling = {"af": af + 1 - 2 * core}

    barrier = pltpu.get_barrier_semaphore()

    def greet_sa(step, carry):
        signal(barrier, {"sa": lax.rem(sa + step, HEADS)})
        return carry

    def greet_af(step, carry):
        signal(barrier, {"af": lax.rem(af + step, ROWS)})
        return carry

    lax.fori_loop(1, HEADS, greet_sa, 0, unroll=True)
    for step in (1, -1, 2, -2):
        signal(barrier, along_z(step))
    lax.fori_loop(1, ROWS, greet_af, 0, unroll=True)

    kv_copy, kv_arrival = exchange("sa", kv_send, kv_recv, kv_ss, kv_rs)
    q_copy, q_arrival = exchange("sa", q_send, q_recv, q_ss, q_rs)
    o_copy, o_arrival = exchange("sa", o_send, o_recv, o_ss, o_rs)
    n_copy, n_arrival = exchange("af", n_send, n_recv, n_ss, n_rs)
    t_copy, t_arrival = exchange("af", t_send, t_recv, t_ss, t_rs)

    own = low * 4 + x

    def columns(j, part):
        return pl.ds(pl.multiple_of((FIRST[j] + TILES[j] * part) * 128, 128), TILES[j] * 128)

    def place(row, rows, j, part):
        return weights.at[pl.ds(pl.multiple_of(row, 16), rows), columns(j, part)]

    def weight_copy(where, send_sem, recv_sem, device):
        return pltpu.make_async_remote_copy(
            src_ref=where,
            dst_ref=where,
            send_sem=send_sem,
            recv_sem=recv_sem,
            device_id=device,
            device_id_type=MESH,
        )

    def unit_copy(u, j, sem, device):
        return weight_copy(place(u * UNIT, UNIT, j, core), sem, unit_rs.at[u, j], device)

    def from_the_left(j):
        return core == (1 if j == 2 else 0)

    def right(u, j):
        return unit_copy(u, j, side_ss.at[0, u, j], along_x(1))

    def left(u, j):
        return unit_copy(u, j, side_ss.at[1, u, j], along_x(-1))

    def up(j):
        return unit_copy(own, j, depth_ss.at[0, j], along_z(1))

    def down(j):
        return unit_copy(own, j, depth_ss.at[1, j], along_z(-1))

    def far(j):
        return unit_copy(own, j, depth_ss.at[2, j], along_z(jnp.where(from_the_left(j), 2, -2)))

    def arrived(u, j):
        unit_copy(u, j, side_ss.at[0, u, j], sibling).wait_recv()

    def unit(low_step, x_step):
        return lax.rem(low + low_step, 4) * 4 + lax.rem(x + x_step, 4)

    def across(g, j, part):
        return weight_copy(
            place(g * GROUP, GROUP, j, part), pair_ss.at[g, j], pair_rs.at[g, j], sibling
        )

    def from_depth(low_step, j):
        u = unit(low_step, 0)
        arrived(u, j)
        right(u, j).start()
        left(u, j).start()

    def from_sides(low_step, j):
        before, after = unit(low_step, 3), unit(low_step, 1)
        arrived(before, j)
        pl.when(from_the_left(j))(lambda: right(before, j).start())
        arrived(after, j)
        pl.when(jnp.logical_not(from_the_left(j)))(lambda: left(after, j).start())

    def complete(low_step, j):
        g = lax.rem(low + low_step, 4)
        arrived(unit(low_step, 2), j)
        across(g, j, core).start()

    def swapped(j):
        for g in range(4):
            across(g, j, 1 - core).wait_recv()

    offsets = (0, TILES[0] * 128, (TILES[0] + TILES[1]) * 128)

    def stage(j):
        return pltpu.make_async_remote_copy(
            src_ref=stage_send.at[:, columns(j, 1 - core)],
            dst_ref=stage_recv.at[:, pl.ds(offsets[j], TILES[j] * 128)],
            send_sem=stage_ss.at[j],
            recv_sem=stage_rs.at[j],
            device_id=sibling,
            device_id_type=MESH,
        )

    stage_send[0:36, 0:D] = out_ref[...]
    stage_send[0:36, D : 4 * D] = temporal_ref[...]
    stage_send[36:48, :] = jnp.zeros((12, 4 * D), BF16)

    for head in range(HEADS):
        base = head * TRIPLE
        for target, row, start in (
            (kv_send, 0, base + HD), (kv_send, PACKED, base + 2 * HD), (q_send, 0, base),
        ):
            top, bottom = packed(x_ref, start)
            target[head, row : row + 64, :] = top
            target[head, row + 64 : row + PACKED, :] = bottom

    pl.semaphore_wait(barrier, HEADS - 1 + ROWS - 1 + 4)
    for j in PIECES:
        stage(j).start()

    def assemble(j):
        width = TILES[j] * 128
        stage(j).wait_recv()
        here = stage_send[0:36, columns(j, core)].astype(F32)
        there = stage_recv[0:36, offsets[j] : offsets[j] + width].astype(F32)
        first = jnp.where(core == 0, here, there)
        second = jnp.where(core == 0, there, here)
        place(own * UNIT, UNIT, j, core)[...] = jnp.concatenate(
            [first, second, jnp.zeros((8, width), F32)], axis=0
        ).astype(BF16)
        for copy in (up, down, far):
            copy(j).start()

    def own_sides(j):
        right(own, j).start()
        left(own, j).start()

    def kv_start(step, carry):
        kv_copy(lax.rem(sa + step, HEADS)).start()
        return carry

    lax.fori_loop(1, HEADS, kv_start, 0, unroll=True)
    for j in PIECES:
        assemble(j)
    for j in PIECES:
        own_sides(j)
    for j in PIECES:
        for low_step in (1, 3, 2):
            from_depth(low_step, j)
    for j in PIECES:
        from_sides(0, j)

    lane = lax.broadcasted_iota(jnp.int32, (TOKENS, 128), 1)

    def take(slot, block):
        key = unpacked(block[0:PACKED])
        value = unpacked(block[PACKED : 2 * PACKED])
        keys[slot] = jnp.where(lane < HD, key, jnp.zeros_like(key))
        values[slot] = jnp.where(lane < HD, value, jnp.ones_like(value))

    take(0, kv_send[sa])
    queries[0] = unpacked(q_send[sa])

    def receive(step, carry):
        source = lax.rem(sa + step, HEADS)
        kv_arrival(source).wait_recv()
        take(step, kv_recv[source])
        kv_copy(source).wait_send()
        q_copy(source).start()
        return carry

    lax.fori_loop(1, HEADS, receive, 0)

    slots = BLOCK // TOKENS

    def attend(block, carry):
        def query(slot):
            source = lax.rem(sa + slot, HEADS)
            q_arrival(source).wait_recv()
            queries[slot] = unpacked(q_recv[source])

        for index in range(slots):
            slot = block * slots + index
            if index == 0:
                pl.when(block > 0)(lambda: query(slot))
            else:
                query(slot)
        rows = queries[pl.ds(block * slots, slots)].reshape(BLOCK, 128)
        all_keys = keys[...].reshape(HEADS * TOKENS, 128)
        all_values = values[...].reshape(HEADS * TOKENS, 128)
        highest = total = None
        for start in range(0, HEADS * TOKENS, CHUNK):
            scores = lax.dot_general(
                rows, all_keys[start : start + CHUNK], (((1,), (1,)), ((), ())),
                preferred_element_type=F32,
            )
            top = jnp.max(scores, axis=-1, keepdims=True)
            if highest is not None:
                top = jnp.maximum(highest, top)
            powers = jnp.exp2((scores - top) * EXP2_SCALE).astype(BF16)
            mixed = jnp.dot(
                powers, all_values[start : start + CHUNK], preferred_element_type=F32
            )
            if highest is not None:
                mixed = mixed + total * jnp.exp2((highest - top) * EXP2_SCALE)
            highest, total = top, mixed
        result = (total / total[:, HD : HD + 1]).astype(BF16)
        for index in range(slots):
            slot = block * slots + index
            owner = lax.rem(sa + slot, HEADS)
            top, bottom = packed(result[index * TOKENS : (index + 1) * TOKENS], 0)
            o_send[owner, 0:64, :] = top
            o_send[owner, 64:PACKED, :] = bottom
            if index == 0:
                pl.when(block > 0)(lambda: o_copy(owner).start())
            else:
                o_copy(owner).start()
        @pl.when(block == 0)
        def _():
            from_sides(1, 0)

        @pl.when(block == 1)
        def _():
            from_sides(1, 1)
            from_sides(1, 2)
            from_sides(3, 0)

        @pl.when(block == 2)
        def _():
            from_sides(3, 1)
            from_sides(3, 2)
            from_sides(2, 0)
            for j in PIECES:
                complete(0, j)

        @pl.when(block == 3)
        def _():
            from_sides(2, 1)
            from_sides(2, 2)
            complete(1, 0)
            complete(1, 1)
            complete(3, 0)

        return carry

    lax.fori_loop(0, HEADS // slots, attend, 0)

    o_recv[sa] = o_send[sa]

    def o_receive(step, carry):
        o_arrival(lax.rem(sa + step, HEADS)).wait_recv()
        return carry

    lax.fori_loop(1, HEADS, o_receive, 0)
    for head in range(HEADS):
        attn[:, head * UNIT : head * UNIT + HD] = unpacked(o_recv[head])[:, 0:HD]
        attn[:, head * UNIT + HD : (head + 1) * UNIT] = jnp.zeros((TOKENS, UNIT - HD), BF16)
    complete(2, 0)
    swapped(0)
    projected = jnp.dot(attn[...], weights[:, 0:D], preferred_element_type=F32)
    hidden = (residual_ref[...].astype(F32) + gate_ref[...].reshape(1, D) * projected).astype(BF16).astype(F32)
    average = jnp.mean(hidden, axis=-1, keepdims=True)
    centred = hidden - average
    variance = jnp.mean(centred * centred, axis=-1, keepdims=True)
    wide[...] = centred * lax.rsqrt(variance + EPSILON)
    to_slabs(slabs, wide)
    n_send[...] = slabs[...].astype(BF16)

    def n_start(step, carry):
        n_copy(lax.rem(af + step, ROWS)).start()
        return carry

    lax.fori_loop(1, ROWS, n_start, 0, unroll=True)
    n_recv[af] = n_send[af]
    complete(3, 1)
    complete(2, 1)
    for low_step in (1, 3, 2):
        complete(low_step, 2)

    def n_receive(step, carry):
        n_arrival(lax.rem(af + step, ROWS)).wait_recv()
        return carry

    lax.fori_loop(1, ROWS, n_receive, 0)
    slabs[...] = n_recv[...].astype(F32)
    from_slabs(dense, slabs)
    for head in range(HEADS):
        attn[:, head * UNIT : head * UNIT + HD] = dense[:, head * HD : (head + 1) * HD]
    swapped(1)
    swapped(2)
    qkv[...] = jnp.dot(attn[...], weights[:, D:], preferred_element_type=F32).astype(BF16)

    first = lax.broadcasted_iota(jnp.int32, (TOKENS, TOKENS), 0)
    second = lax.broadcasted_iota(jnp.int32, (TOKENS, TOKENS), 1)
    same = lax.shift_right_logical(first, 5) == lax.shift_right_logical(second, 5)
    outside = jnp.where(same, 0.0, -jnp.inf).astype(F32)

    def temporal_scores(head):
        base = head * TRIPLE
        return outside + lax.dot_general(
            qkv[:, base : base + HD], qkv[:, base + HD : base + 2 * HD],
            (((1,), (1,)), ((), ())), preferred_element_type=F32,
        )

    def temporal_shares(scores):
        highest = jnp.max(scores, axis=-1, keepdims=True)
        powers = jnp.exp2((scores - highest) * EXP2_SCALE)
        return (powers / jnp.sum(powers, axis=-1, keepdims=True)).astype(BF16)

    for pair in range(0, HEADS, 2):
        heads = (pair, pair + 1)
        scores = [temporal_scores(head) for head in heads]
        shares = [temporal_shares(score) for score in scores]
        for head, share in zip(heads, shares):
            base = head * TRIPLE
            wide[:, head * HD : (head + 1) * HD] = jnp.dot(
                share, qkv[:, base + 2 * HD : base + 3 * HD], preferred_element_type=F32
            )
    to_slabs(slabs, wide)
    t_send[...] = slabs[...].astype(BF16)

    def t_start(step, carry):
        t_copy(lax.rem(af + step, ROWS)).start()
        return carry

    lax.fori_loop(1, ROWS, t_start, 0, unroll=True)
    t_recv[af] = t_send[af]

    def drain_sa(step, carry):
        peer = lax.rem(sa + step, HEADS)
        q_copy(peer).wait_send()
        o_copy(peer).wait_send()
        return carry

    lax.fori_loop(1, HEADS, drain_sa, 0)
    for j in PIECES:
        stage(j).wait_send()
        for copy in (up, down, far):
            copy(j).wait_send()

    def drain_weights(turn, carry):
        for j in PIECES:
            right(unit(turn, 0), j).wait_send()
            left(unit(turn, 0), j).wait_send()
            pl.when(from_the_left(j))(lambda: right(unit(turn, 3), j).wait_send())
            pl.when(jnp.logical_not(from_the_left(j)))(lambda: left(unit(turn, 1), j).wait_send())
            across(turn, j, core).wait_send()
        return carry

    lax.fori_loop(0, 4, drain_weights, 0)

    def t_receive(step, carry):
        peer = lax.rem(af + step, ROWS)
        n_copy(peer).wait_send()
        t_arrival(peer).wait_recv()
        return carry

    lax.fori_loop(1, ROWS, t_receive, 0)
    slabs[...] = t_recv[...].astype(F32)
    from_slabs(o_ref, slabs)

    def drain_af(step, carry):
        t_copy(lax.rem(af + step, ROWS)).wait_send()
        return carry

    lax.fori_loop(1, ROWS, drain_af, 0)


def flat(values):
    return jnp.transpose(values, (0, 2, 1, 3)).reshape(-1, values.shape[-1])


def local(spatial_qkv, residual, gate, out_weight, temporal_weight):
    frames, rows, cols, _ = residual.shape
    dma = pltpu.SemaphoreType.DMA
    attended = pl.pallas_call(
        kernel,
        out_shape=jax.ShapeDtypeStruct((TOKENS, D), BF16),
        in_specs=[pl.BlockSpec(memory_space=pltpu.VMEM)] * 5,
        out_specs=pl.BlockSpec(memory_space=pltpu.VMEM),
        scratch_shapes=[
            pltpu.VMEM((HEADS, 2 * PACKED, 128), BF16),
            pltpu.VMEM((HEADS, 2 * PACKED, 128), BF16),
            pltpu.VMEM((HEADS, PACKED, 128), BF16),
            pltpu.VMEM((HEADS, PACKED, 128), BF16),
            pltpu.VMEM((HEADS, PACKED, 128), BF16),
            pltpu.VMEM((HEADS, PACKED, 128), BF16),
            pltpu.VMEM((HEADS, TOKENS, 128), BF16),
            pltpu.VMEM((HEADS, TOKENS, 128), BF16),
            pltpu.VMEM((HEADS, TOKENS, 128), BF16),
            pltpu.VMEM((TOKENS, HEADS * UNIT), BF16),
            pltpu.VMEM((HEADS * UNIT, 4 * D), BF16),
            pltpu.VMEM((48, 4 * D), BF16),
            pltpu.VMEM((48, sum(TILES) * 128), BF16),
            pltpu.VMEM((ROWS, SLABS, 128), F32),
            pltpu.VMEM((ROWS, SLABS, 128), BF16),
            pltpu.VMEM((ROWS, SLABS, 128), BF16),
            pltpu.VMEM((TOKENS, D), F32),
            pltpu.VMEM((TOKENS, D), BF16),
            pltpu.VMEM((TOKENS, 3 * D), BF16),
            pltpu.VMEM((ROWS, SLABS, 128), BF16),
            pltpu.VMEM((ROWS, SLABS, 128), BF16),
        ]
        + [dma((HEADS,))] * 6
        + [dma((ROWS,))] * 4
        + [
            dma((3,)), dma((3,)), dma((3, 3)), dma((2, 16, 3)), dma((16, 3)),
            dma((4, 3)), dma((4, 3)),
        ],
        compiler_params=pltpu.CompilerParams(
            collective_id=0, has_side_effects=True, vmem_limit_bytes=VMEM_LIMIT
        ),
    )(flat(spatial_qkv), flat(residual), gate, out_weight, temporal_weight)
    return jnp.transpose(attended.reshape(frames, cols, rows, D), (0, 2, 1, 3))


def solution(mesh):
    placed = (
        P("af", None, "sa", None),
        P("af", None, "sa", None),
        P(),
        P("af", None),
        P("af", None),
    )
    return jax.shard_map(
        local, mesh=mesh, in_specs=placed, out_specs=P("af", None, "sa", None), check_vma=False
    )
```

```python
import math

import jax
import jax.numpy as jnp
from jax import lax
from jax.experimental import pallas as pl
from jax.experimental.pallas import tpu as pltpu
from jax.sharding import PartitionSpec as P

D = 1152
HEADS = 16
HD = 72
TRIPLE = 3 * HD
EPSILON = 1e-06
SCALE = 1.0 / math.sqrt(HD)
EXP2_SCALE = SCALE * math.log2(math.e)
MESH = pl.DeviceIdType.MESH
F32 = jnp.float32
BF16 = jnp.bfloat16
VMEM_LIMIT = 60 * 1024 * 1024

ROWS = 32
COLS = 5
TOKENS = ROWS * COLS
SLABS = 48
PACKED = 96
UNIT = 80
BLOCK = 640
CHUNK = 256
FIRST = (0, 10, 18)
TILES = (5, 4, 9)
PIECES = range(3)
GROUP = 4 * UNIT


def signal(barrier, device):
    pl.semaphore_signal(barrier, inc=1, device_id=device, device_id_type=MESH)


def exchange(axis, source, target, send_sem, recv_sem):
    me = lax.axis_index(axis)

    def describe(peer, slot):
        return pltpu.make_async_remote_copy(
            src_ref=source.at[peer],
            dst_ref=target.at[slot],
            send_sem=send_sem.at[peer],
            recv_sem=recv_sem.at[slot],
            device_id={axis: peer},
            device_id_type=MESH,
        )

    return lambda peer: describe(peer, me), lambda peer: describe(peer, peer)


def packed(values, base):
    top = jnp.concatenate(
        [values[0:64, base : base + HD], values[96:160, base : base + 56]], axis=1
    )
    bottom = jnp.concatenate(
        [
            values[64:96, base : base + HD],
            values[96:128, base + 56 : base + HD],
            values[128:160, base + 56 : base + HD],
            jnp.zeros((32, 24), values.dtype),
        ],
        axis=1,
    )
    return top, bottom


def unpacked(block):
    rest = jnp.zeros((32, 56), block.dtype)
    third = jnp.concatenate([block[0:32, HD:128], block[64:96, HD : HD + 16], rest], axis=1)
    fourth = jnp.concatenate(
        [block[32:64, HD:128], block[64:96, HD + 16 : HD + 32], rest], axis=1
    )
    return jnp.concatenate([block, third, fourth], axis=0)


def to_slabs(slabs, values):
    for col in range(COLS):
        for part in range(D // 128):
            slabs[:, col * 9 + part, :] = values[
                col * ROWS : (col + 1) * ROWS, part * 128 : (part + 1) * 128
            ]
    slabs[:, COLS * 9 : SLABS, :] = jnp.zeros((ROWS, SLABS - COLS * 9, 128), F32)


def from_slabs(target, slabs):
    for col in range(COLS):
        for part in range(D // 128):
            target[col * ROWS : (col + 1) * ROWS, part * 128 : (part + 1) * 128] = slabs[
                :, col * 9 + part, :
            ].astype(BF16)


def kernel(
    x_ref, residual_ref, gate_ref, out_ref, temporal_ref, o_ref,
    kv_send, kv_recv, q_send, q_recv, o_send, o_recv, queries, keys, values, attn,
    weights, stage_send, stage_recv,
    slabs, n_send, n_recv, wide, dense, qkv, t_send, t_recv,
    kv_ss, kv_rs, q_ss, q_rs, o_ss, o_rs, n_ss, n_rs, t_ss, t_rs,
    stage_ss, stage_rs, depth_ss, side_ss, unit_rs, pair_ss, pair_rs,
):
    af, sa = lax.axis_index("af"), lax.axis_index("sa")
    low, x, core = lax.div(af, 8), lax.rem(lax.div(af, 2), 4), lax.rem(af, 2)
    high, y = lax.div(sa, 8), lax.rem(sa, 8)
    z = high * 4 + low

    def along_z(step):
        there = lax.rem(z + step + 8, 8)
        return {
            "af": lax.rem(there, 4) * 8 + x * 2 + core,
            "sa": lax.div(there, 4) * 8 + y,
        }

    def along_x(step):
        return {"af": low * 8 + lax.rem(x + step + 4, 4) * 2 + core}

    sibling = {"af": af + 1 - 2 * core}

    barrier = pltpu.get_barrier_semaphore()

    def greet_sa(step, carry):
        signal(barrier, {"sa": lax.rem(sa + step, HEADS)})
        return carry

    def greet_af(step, carry):
        signal(barrier, {"af": lax.rem(af + step, ROWS)})
        return carry

    lax.fori_loop(1, HEADS, greet_sa, 0, unroll=True)
    for step in (1, -1, 2, -2):
        signal(barrier, along_z(step))
    lax.fori_loop(1, ROWS, greet_af, 0, unroll=True)

    kv_copy, kv_arrival = exchange("sa", kv_send, kv_recv, kv_ss, kv_rs)
    q_copy, q_arrival = exchange("sa", q_send, q_recv, q_ss, q_rs)
    o_copy, o_arrival = exchange("sa", o_send, o_recv, o_ss, o_rs)
    n_copy, n_arrival = exchange("af", n_send, n_recv, n_ss, n_rs)
    t_copy, t_arrival = exchange("af", t_send, t_recv, t_ss, t_rs)

    own = low * 4 + x

    def columns(j, part):
        return pl.ds(pl.multiple_of((FIRST[j] + TILES[j] * part) * 128, 128), TILES[j] * 128)

    def place(row, rows, j, part):
        return weights.at[pl.ds(pl.multiple_of(row, 16), rows), columns(j, part)]

    def weight_copy(where, send_sem, recv_sem, device):
        return pltpu.make_async_remote_copy(
            src_ref=where,
            dst_ref=where,
            send_sem=send_sem,
            recv_sem=recv_sem,
            device_id=device,
            device_id_type=MESH,
        )

    def unit_copy(u, j, sem, device):
        return weight_copy(place(u * UNIT, UNIT, j, core), sem, unit_rs.at[u, j], device)

    def from_the_left(j):
        return core == (1 if j == 2 else 0)

    def right(u, j):
        return unit_copy(u, j, side_ss.at[0, u, j], along_x(1))

    def left(u, j):
        return unit_copy(u, j, side_ss.at[1, u, j], along_x(-1))

    def up(j):
        return unit_copy(own, j, depth_ss.at[0, j], along_z(1))

    def down(j):
        return unit_copy(own, j, depth_ss.at[1, j], along_z(-1))

    def far(j):
        return unit_copy(own, j, depth_ss.at[2, j], along_z(jnp.where(from_the_left(j), 2, -2)))

    def arrived(u, j):
        unit_copy(u, j, side_ss.at[0, u, j], sibling).wait_recv()

    def unit(low_step, x_step):
        return lax.rem(low + low_step, 4) * 4 + lax.rem(x + x_step, 4)

    def across(g, j, part):
        return weight_copy(
            place(g * GROUP, GROUP, j, part), pair_ss.at[g, j], pair_rs.at[g, j], sibling
        )

    def from_depth(low_step, j):
        u = unit(low_step, 0)
        arrived(u, j)
        right(u, j).start()
        left(u, j).start()

    def from_sides(low_step, j):
        before, after = unit(low_step, 3), unit(low_step, 1)
        arrived(before, j)
        pl.when(from_the_left(j))(lambda: right(before, j).start())
        arrived(after, j)
        pl.when(jnp.logical_not(from_the_left(j)))(lambda: left(after, j).start())

    def complete(low_step, j):
        g = lax.rem(low + low_step, 4)
        arrived(unit(low_step, 2), j)
        across(g, j, core).start()

    def swapped(j):
        for g in range(4):
            across(g, j, 1 - core).wait_recv()

    offsets = (0, TILES[0] * 128, (TILES[0] + TILES[1]) * 128)

    def stage(j):
        return pltpu.make_async_remote_copy(
            src_ref=stage_send.at[:, columns(j, 1 - core)],
            dst_ref=stage_recv.at[:, pl.ds(offsets[j], TILES[j] * 128)],
            send_sem=stage_ss.at[j],
            recv_sem=stage_rs.at[j],
            device_id=sibling,
            device_id_type=MESH,
        )

    stage_send[0:36, 0:D] = out_ref[...]
    stage_send[0:36, D : 4 * D] = temporal_ref[...]
    stage_send[36:48, :] = jnp.zeros((12, 4 * D), BF16)

    for head in range(HEADS):
        base = head * TRIPLE
        for target, row, start in (
            (kv_send, 0, base + HD), (kv_send, PACKED, base + 2 * HD), (q_send, 0, base),
        ):
            top, bottom = packed(x_ref, start)
            target[head, row : row + 64, :] = top
            target[head, row + 64 : row + PACKED, :] = bottom

    pl.semaphore_wait(barrier, HEADS - 1 + ROWS - 1 + 4)
    for j in PIECES:
        stage(j).start()

    def assemble(j):
        width = TILES[j] * 128
        stage(j).wait_recv()
        here = stage_send[0:36, columns(j, core)].astype(F32)
        there = stage_recv[0:36, offsets[j] : offsets[j] + width].astype(F32)
        first = jnp.where(core == 0, here, there)
        second = jnp.where(core == 0, there, here)
        place(own * UNIT, UNIT, j, core)[...] = jnp.concatenate(
            [first, second, jnp.zeros((8, width), F32)], axis=0
        ).astype(BF16)
        for copy in (up, down, far):
            copy(j).start()

    def own_sides(j):
        right(own, j).start()
        left(own, j).start()

    def kv_start(step, carry):
        kv_copy(lax.rem(sa + step, HEADS)).start()
        return carry

    lax.fori_loop(1, HEADS, kv_start, 0, unroll=True)
    for j in PIECES:
        assemble(j)
    for j in PIECES:
        own_sides(j)
    for j in PIECES:
        for low_step in (1, 3, 2):
            from_depth(low_step, j)
    for j in PIECES:
        from_sides(0, j)

    lane = lax.broadcasted_iota(jnp.int32, (TOKENS, 128), 1)

    def take(slot, block):
        key = unpacked(block[0:PACKED])
        value = unpacked(block[PACKED : 2 * PACKED])
        keys[slot] = jnp.where(lane < HD, key, jnp.zeros_like(key))
        values[slot] = jnp.where(lane < HD, value, jnp.ones_like(value))

    take(0, kv_send[sa])
    queries[0] = unpacked(q_send[sa])

    def receive(step, carry):
        source = lax.rem(sa + step, HEADS)
        kv_arrival(source).wait_recv()
        take(step, kv_recv[source])
        kv_copy(source).wait_send()
        q_copy(source).start()
        return carry

    lax.fori_loop(1, HEADS, receive, 0)

    slots = BLOCK // TOKENS

    def attend(block, carry):
        def query(slot):
            source = lax.rem(sa + slot, HEADS)
            q_arrival(source).wait_recv()
            queries[slot] = unpacked(q_recv[source])

        for index in range(slots):
            slot = block * slots + index
            if index == 0:
                pl.when(block > 0)(lambda: query(slot))
            else:
                query(slot)
        rows = queries[pl.ds(block * slots, slots)].reshape(BLOCK, 128)
        all_keys = keys[...].reshape(HEADS * TOKENS, 128)
        all_values = values[...].reshape(HEADS * TOKENS, 128)
        highest = total = None
        for start in range(0, HEADS * TOKENS, CHUNK):
            scores = lax.dot_general(
                rows, all_keys[start : start + CHUNK], (((1,), (1,)), ((), ())),
                preferred_element_type=F32,
            )
            top = jnp.max(scores, axis=-1, keepdims=True)
            if highest is not None:
                top = jnp.maximum(highest, top)
            powers = jnp.exp2((scores - top) * EXP2_SCALE).astype(BF16)
            mixed = jnp.dot(
                powers, all_values[start : start + CHUNK], preferred_element_type=F32
            )
            if highest is not None:
                mixed = mixed + total * jnp.exp2((highest - top) * EXP2_SCALE)
            highest, total = top, mixed
        result = (total / total[:, HD : HD + 1]).astype(BF16)
        for index in range(slots):
            slot = block * slots + index
            owner = lax.rem(sa + slot, HEADS)
            top, bottom = packed(result[index * TOKENS : (index + 1) * TOKENS], 0)
            o_send[owner, 0:64, :] = top
            o_send[owner, 64:PACKED, :] = bottom
            if index == 0:
                pl.when(block > 0)(lambda: o_copy(owner).start())
            else:
                o_copy(owner).start()
        @pl.when(block == 0)
        def _():
            from_sides(1, 0)

        @pl.when(block == 1)
        def _():
            from_sides(1, 1)
            from_sides(1, 2)
            from_sides(3, 0)

        @pl.when(block == 2)
        def _():
            from_sides(3, 1)
            from_sides(3, 2)
            from_sides(2, 0)
            for j in PIECES:
                complete(0, j)

        @pl.when(block == 3)
        def _():
            from_sides(2, 1)
            from_sides(2, 2)
            complete(1, 0)
            complete(1, 1)
            complete(3, 0)

        return carry

    lax.fori_loop(0, HEADS // slots, attend, 0)

    o_recv[sa] = o_send[sa]

    def o_receive(step, carry):
        o_arrival(lax.rem(sa + step, HEADS)).wait_recv()
        return carry

    lax.fori_loop(1, HEADS, o_receive, 0, unroll=True)
    for head in range(HEADS):
        attn[:, head * UNIT : head * UNIT + HD] = unpacked(o_recv[head])[:, 0:HD]
        attn[:, head * UNIT + HD : (head + 1) * UNIT] = jnp.zeros((TOKENS, UNIT - HD), BF16)
    complete(2, 0)
    swapped(0)
    projected = jnp.dot(attn[...], weights[:, 0:D], preferred_element_type=F32)
    hidden = (residual_ref[...].astype(F32) + gate_ref[...].reshape(1, D) * projected).astype(BF16).astype(F32)
    average = jnp.mean(hidden, axis=-1, keepdims=True)
    centred = hidden - average
    variance = jnp.mean(centred * centred, axis=-1, keepdims=True)
    wide[...] = centred * lax.rsqrt(variance + EPSILON)
    to_slabs(slabs, wide)
    n_send[...] = slabs[...].astype(BF16)

    def n_start(step, carry):
        n_copy(lax.rem(af + step, ROWS)).start()
        return carry

    lax.fori_loop(1, ROWS, n_start, 0, unroll=True)
    n_recv[af] = n_send[af]
    complete(3, 1)
    complete(2, 1)
    for low_step in (1, 3, 2):
        complete(low_step, 2)

    def n_receive(step, carry):
        n_arrival(lax.rem(af + step, ROWS)).wait_recv()
        return carry

    lax.fori_loop(1, ROWS, n_receive, 0, unroll=True)
    slabs[...] = n_recv[...].astype(F32)
    from_slabs(dense, slabs)
    for head in range(HEADS):
        attn[:, head * UNIT : head * UNIT + HD] = dense[:, head * HD : (head + 1) * HD]
    swapped(1)
    swapped(2)
    qkv[...] = jnp.dot(attn[...], weights[:, D:], preferred_element_type=F32).astype(BF16)

    first = lax.broadcasted_iota(jnp.int32, (TOKENS, TOKENS), 0)
    second = lax.broadcasted_iota(jnp.int32, (TOKENS, TOKENS), 1)
    same = lax.shift_right_logical(first, 5) == lax.shift_right_logical(second, 5)
    outside = jnp.where(same, 0.0, -jnp.inf).astype(F32)

    def temporal_scores(head):
        base = head * TRIPLE
        return outside + lax.dot_general(
            qkv[:, base : base + HD], qkv[:, base + HD : base + 2 * HD],
            (((1,), (1,)), ((), ())), preferred_element_type=F32,
        )

    def temporal_shares(scores):
        highest = jnp.max(scores, axis=-1, keepdims=True)
        powers = jnp.exp2((scores - highest) * EXP2_SCALE)
        return (powers / jnp.sum(powers, axis=-1, keepdims=True)).astype(BF16)

    for pair in range(0, HEADS, 2):
        heads = (pair, pair + 1)
        scores = [temporal_scores(head) for head in heads]
        shares = [temporal_shares(score) for score in scores]
        for head, share in zip(heads, shares):
            base = head * TRIPLE
            wide[:, head * HD : (head + 1) * HD] = jnp.dot(
                share, qkv[:, base + 2 * HD : base + 3 * HD], preferred_element_type=F32
            )
    to_slabs(slabs, wide)
    t_send[...] = slabs[...].astype(BF16)

    def t_start(step, carry):
        t_copy(lax.rem(af + step, ROWS)).start()
        return carry

    lax.fori_loop(1, ROWS, t_start, 0, unroll=True)
    t_recv[af] = t_send[af]

    def drain_sa(step, carry):
        peer = lax.rem(sa + step, HEADS)
        q_copy(peer).wait_send()
        o_copy(peer).wait_send()
        return carry

    lax.fori_loop(1, HEADS, drain_sa, 0, unroll=True)
    for j in PIECES:
        stage(j).wait_send()
        for copy in (up, down, far):
            copy(j).wait_send()

    def drain_weights(turn, carry):
        for j in PIECES:
            right(unit(turn, 0), j).wait_send()
            left(unit(turn, 0), j).wait_send()
            pl.when(from_the_left(j))(lambda: right(unit(turn, 3), j).wait_send())
            pl.when(jnp.logical_not(from_the_left(j)))(lambda: left(unit(turn, 1), j).wait_send())
            across(turn, j, core).wait_send()
        return carry

    lax.fori_loop(0, 4, drain_weights, 0)

    def t_receive(step, carry):
        peer = lax.rem(af + step, ROWS)
        n_copy(peer).wait_send()
        t_arrival(peer).wait_recv()
        return carry

    lax.fori_loop(1, ROWS, t_receive, 0, unroll=True)
    slabs[...] = t_recv[...].astype(F32)
    from_slabs(o_ref, slabs)

    def drain_af(step, carry):
        t_copy(lax.rem(af + step, ROWS)).wait_send()
        return carry

    lax.fori_loop(1, ROWS, drain_af, 0, unroll=True)


def flat(values):
    return jnp.transpose(values, (0, 2, 1, 3)).reshape(-1, values.shape[-1])


def local(spatial_qkv, residual, gate, out_weight, temporal_weight):
    frames, rows, cols, _ = residual.shape
    dma = pltpu.SemaphoreType.DMA
    attended = pl.pallas_call(
        kernel,
        out_shape=jax.ShapeDtypeStruct((TOKENS, D), BF16),
        in_specs=[pl.BlockSpec(memory_space=pltpu.VMEM)] * 5,
        out_specs=pl.BlockSpec(memory_space=pltpu.VMEM),
        scratch_shapes=[
            pltpu.VMEM((HEADS, 2 * PACKED, 128), BF16),
            pltpu.VMEM((HEADS, 2 * PACKED, 128), BF16),
            pltpu.VMEM((HEADS, PACKED, 128), BF16),
            pltpu.VMEM((HEADS, PACKED, 128), BF16),
            pltpu.VMEM((HEADS, PACKED, 128), BF16),
            pltpu.VMEM((HEADS, PACKED, 128), BF16),
            pltpu.VMEM((HEADS, TOKENS, 128), BF16),
            pltpu.VMEM((HEADS, TOKENS, 128), BF16),
            pltpu.VMEM((HEADS, TOKENS, 128), BF16),
            pltpu.VMEM((TOKENS, HEADS * UNIT), BF16),
            pltpu.VMEM((HEADS * UNIT, 4 * D), BF16),
            pltpu.VMEM((48, 4 * D), BF16),
            pltpu.VMEM((48, sum(TILES) * 128), BF16),
            pltpu.VMEM((ROWS, SLABS, 128), F32),
            pltpu.VMEM((ROWS, SLABS, 128), BF16),
            pltpu.VMEM((ROWS, SLABS, 128), BF16),
            pltpu.VMEM((TOKENS, D), F32),
            pltpu.VMEM((TOKENS, D), BF16),
            pltpu.VMEM((TOKENS, 3 * D), BF16),
            pltpu.VMEM((ROWS, SLABS, 128), BF16),
            pltpu.VMEM((ROWS, SLABS, 128), BF16),
        ]
        + [dma((HEADS,))] * 6
        + [dma((ROWS,))] * 4
        + [
            dma((3,)), dma((3,)), dma((3, 3)), dma((2, 16, 3)), dma((16, 3)),
            dma((4, 3)), dma((4, 3)),
        ],
        compiler_params=pltpu.CompilerParams(
            collective_id=0, has_side_effects=True, vmem_limit_bytes=VMEM_LIMIT
        ),
    )(flat(spatial_qkv), flat(residual), gate, out_weight, temporal_weight)
    return jnp.transpose(attended.reshape(frames, cols, rows, D), (0, 2, 1, 3))


def solution(mesh):
    placed = (
        P("af", None, "sa", None),
        P("af", None, "sa", None),
        P(),
        P("af", None),
        P("af", None),
    )
    return jax.shard_map(
        local, mesh=mesh, in_specs=placed, out_specs=P("af", None, "sa", None), check_vma=False
    )
```
